32 devices in a mesh: pos: 2 (over core), rows: 16 (over z, y, x).
Axes of the slice: x: 2, y: 2, z: 4, core: 2. Of those that a mesh axis runs over, the one named last changes fastest.
Arguments:
- matrix: float32 [8192, 512], P('rows', 'pos'), may hold values from -40 to 40
- shifts: int32 [3], replicated, may hold values from 1 to 7, as said below
Outputs:
- rotated: float32 [8192, 512], P('rows', 'pos')
The draws below stay inside these ranges and needn't reach their ends.
Inputs may be any that keep to these rules, and one draw needn't show every extreme that they name: `shifts`: each entry is a distance between pair positions, taken modulo 2; 7 and 1 both occur in every draw.
All inputs are finite; a program needn't handle non-finite values. Where the reference program divides by a largest or mean magnitude, that divisor is 1e-20 or more.
Results may differ from the reference program's by a relative error of at most 0.00018.
Values sent between devices are 32-bit elements; how exact they have to be, the bound alone decides.
No kernel may reach another device: no remote copies, remote signals or barrier semaphores. Data moves between devices by JAX's collectives and lax.ppermute only.
A program may use at most 64 MiB of HBM per device.

```python
import jax
import jax.numpy as jnp
from jax import lax

BLK = 128
ROW_DEV = 512
ROUNDS = 3
NS_STEPS = 3
N_POS = 2
N_ROWS = 16


def draw_matrix(key, part):
    keys = jax.random.split(jax.random.fold_in(key, 11), 4)
    total_rows = ROW_DEV * N_ROWS
    total_cols = 2 * BLK * N_POS
    col_scale = jnp.exp(jax.random.uniform(keys[0], (1, total_cols), jnp.float32, jnp.log(0.3), jnp.log(3.0)))
    factor_rows = jnp.clip(jax.random.normal(keys[1], (total_rows, 1), jnp.float32), -3.0, 3.0)
    factor_cols = jnp.clip(jax.random.normal(keys[2], (1, total_cols), jnp.float32), -3.0, 3.0)
    noise = jnp.clip(jax.random.normal(keys[3], (total_rows, total_cols), jnp.float32), -4.0, 4.0)
    common = 0.7
    return col_scale * (noise + common * factor_rows * factor_cols)


def draw_shifts(key, part):
    keys = jax.random.split(jax.random.fold_in(key, 23), 2)
    values = jax.random.randint(keys[0], (ROUNDS,), 1, 4 * N_POS)
    order = jax.random.permutation(keys[1], ROUNDS)
    slots = jnp.arange(ROUNDS)
    values = jnp.where(slots == order[0], 4 * N_POS - 1, values)
    values = jnp.where(slots == order[1], N_POS - 1, values)
    return values.astype(jnp.int32)


def setup_inputs(seed: int = 0) -> dict:
    key_list = jax.random.split(jax.random.key(seed), 3)
    matrix = draw_matrix(jax.random.fold_in(key_list[2], 71), 0)
    shifts = draw_shifts(jax.random.fold_in(key_list[2], 71), 0)
    return dict(matrix=matrix, shifts=shifts)


def product(left, right):
    return jnp.dot(left, right, precision=lax.Precision.HIGHEST, preferred_element_type=jnp.float32)

def rotation(gram_matrix):
    width = gram_matrix.shape[0]
    identity = jnp.eye(width, dtype=gram_matrix.dtype)
    inverse_norm = 1.0 / jnp.sqrt(jnp.diagonal(gram_matrix) + 1e-06)
    scaled = gram_matrix * inverse_norm[:, None] * inverse_norm[None, :]
    upper = jnp.triu(scaled, 1)
    skew_raw = upper - upper.T
    bound_value = jnp.max(lax.optimization_barrier(jnp.sum(jnp.abs(skew_raw), axis=1)))
    skew = skew_raw / (1.0 + 2.0 * bound_value)
    shifted = identity - skew
    inverse = identity + skew
    for step in range(NS_STEPS):
        inverse = product(inverse, 2.0 * identity - product(shifted, inverse))
    return product(inverse, identity + skew)

def one_position(block):
    gram_matrix = product(block.T, block)
    return product(block, rotation(gram_matrix))

def reference(matrix, shifts):
    rows_total = matrix.shape[0]
    current = matrix.reshape(rows_total, N_POS, 2 * BLK).transpose(1, 0, 2)
    for round_index in range(ROUNDS):
        current = lax.map(one_position, current)
        moved = jnp.roll(current[:, :, BLK:], shifts[round_index], axis=0)
        current = jnp.concatenate([current[:, :, :BLK], moved], axis=2)
    return current.transpose(1, 0, 2).reshape(rows_total, N_POS * 2 * BLK)
```

```python
import functools

import jax
import jax.numpy as jnp
from jax import lax
from jax.experimental import pallas as pl
from jax.experimental.pallas import tpu as pltpu
from jax.sharding import PartitionSpec as P

ROUNDS = 3
NS_STEPS = 3
EXTRA = 8
F32 = jnp.float32
BF16 = jnp.bfloat16
VMEM = pl.BlockSpec(memory_space=pltpu.VMEM)
SMEM = pl.BlockSpec(memory_space=pltpu.SMEM)


def from_behind(x, axis, by):
    size = lax.axis_size(axis)
    return lax.ppermute(x, axis, [(i, (i + by) % size) for i in range(size)])


def product(left, right):
    return jnp.dot(left, right, precision=lax.Precision.HIGHEST, preferred_element_type=F32)


def rotation(gram_matrix):
    width = gram_matrix.shape[0]
    identity = jnp.eye(width, dtype=gram_matrix.dtype)
    inverse_norm = 1.0 / jnp.sqrt(jnp.diagonal(gram_matrix) + 1e-06)
    scaled = gram_matrix * inverse_norm[:, None] * inverse_norm[None, :]
    upper = jnp.triu(scaled, 1)
    skew_raw = upper - upper.T
    bound_value = jnp.max(jnp.sum(jnp.abs(skew_raw), axis=1))
    skew = skew_raw / (1.0 + 2.0 * bound_value)
    shifted = identity - skew
    inverse = identity + skew
    for step in range(NS_STEPS):
        inverse = product(inverse, 2.0 * identity - product(shifted, inverse))
    return product(inverse, identity + skew)


def make_branch(step_size):

    def moved(block):
        if step_size == 0:
            return block
        return from_behind(block, "pos", step_size)

    return moved


def shards(matrix, shifts):
    current = matrix
    half = current.shape[1] // 2
    position_count = lax.axis_size("pos")
    for round_index in range(ROUNDS):
        gram_matrix = lax.psum(product(current.T, current), "rows")
        current = product(current, rotation(gram_matrix))
        distance = shifts[round_index] % position_count
        first_cols = current[:, :half]
        second_cols = current[:, half:]
        branches = [make_branch(step_size) for step_size in range(position_count)]
        second_cols = lax.switch(distance, branches, second_cols)
        current = jnp.concatenate([first_cols, second_cols], axis=1)
    return current


def split(x):
    high = x.astype(BF16)
    return high, (x - high.astype(F32)).astype(BF16)


def dot(left, right, contract=1):
    return lax.dot_general(
        left, right, (((contract,), (0,)), ((), ())), preferred_element_type=F32
    )


def dot3(left, right, contract=1):
    (left_high, left_low), (right_high, right_low) = left, right
    return (
        dot(left_high, right_low, contract)
        + dot(left_low, right_high, contract)
        + dot(left_high, right_high, contract)
    )


def gram_kernel(where, own, other, *refs):
    outs, (high, low, blocks) = refs[:4], refs[4:]
    half = own.shape[1] // 2
    position, corner = where[0], where[1]
    for ref, place in ((own, position), (other, 1 - position)):
        part = split(ref[...])
        high[place], low[place] = part
    mine = high[position], low[position]
    gram = dot3(mine, mine, 0)
    columns = pl.ds(pl.multiple_of(position * half, half), half)
    cross = dot3((high[0], low[0]), (high[1, :, columns], low[1, :, columns]), 0)
    first, second = gram[:half, :half], gram[half:, half:]
    row = lax.broadcasted_iota(jnp.int32, (half, half), 0)
    col = lax.broadcasted_iota(jnp.int32, (half, half), 1)
    blocks[0, :half] = jnp.where(col >= row, first, second)
    diagonal = jnp.sum(jnp.where(col == row, second, 0.0), axis=0, keepdims=True)
    blocks[0, half:] = jnp.broadcast_to(diagonal, (EXTRA, half))
    blocks[1, :half] = gram[:half, half:]
    blocks[2, :half] = cross[:half]
    blocks[3, :half] = cross[half:]
    for slot in (1, 2, 3):
        blocks[slot, half:] = jnp.zeros((EXTRA, half), F32)
    for offset, out in enumerate(outs):
        out[...] = blocks[corner ^ offset]


def sum_kernel(*refs):
    ins, out = refs[:-1], refs[-1]
    total = ins[0][...]
    for ref in ins[1:]:
        total = total + ref[...]
    out[...] = total


def symmetric(block, extra):
    half = block.shape[0]
    row = lax.broadcasted_iota(jnp.int32, (half, half), 0)
    col = lax.broadcasted_iota(jnp.int32, (half, half), 1)
    turned = block.T
    first = jnp.where(col >= row, block, turned)
    second = jnp.where(col > row, turned, jnp.where(col < row, block, extra[:1]))
    return first, second


def beside(left, right):
    return jnp.concatenate([left, right], axis=1)


def above(top, bottom):
    return jnp.concatenate([top, bottom], axis=0)


def cayley_of(gram):
    width = gram.shape[0]
    row = lax.broadcasted_iota(jnp.int32, (width, width), 0)
    col = lax.broadcasted_iota(jnp.int32, (width, width), 1)
    on_diagonal = row == col
    diagonal = jnp.where(on_diagonal, gram, 0.0)
    inverse_row = 1.0 / jnp.sqrt(jnp.sum(diagonal, axis=0, keepdims=True) + 1e-06)
    inverse_col = 1.0 / jnp.sqrt(jnp.sum(diagonal, axis=1, keepdims=True) + 1e-06)
    scaled = gram * inverse_col * inverse_row
    raw = jnp.where(on_diagonal, 0.0, jnp.where(col > row, scaled, -scaled))
    bound = jnp.max(jnp.sum(jnp.abs(raw), axis=0, keepdims=True), axis=1, keepdims=True)
    skew = raw / (1.0 + 2.0 * bound)
    identity = jnp.where(on_diagonal, 1.0, 0.0)
    skew_parts = split(skew)
    square = dot3(skew_parts, skew_parts)
    square_parts = split(square)
    cube = dot3(skew_parts, square_parts)
    fourth = dot3(square_parts, square_parts)
    fourth_parts = split(fourth)
    base = identity + 2.0 * (skew + square + cube) + fourth
    eighth = dot(fourth_parts[0], fourth_parts[0])
    base = base + dot3(split(base), fourth_parts)
    return base + dot(base.astype(BF16), eighth.astype(BF16))


def rounds_kernel(scalars, *refs):
    mine, theirs, (own, other), out = refs[:4], refs[4:8], refs[8:10], refs[10]
    pieces, high, low, turn_high, turn_low = refs[11:]
    position, corner = scalars[0], scalars[1]
    half = own.shape[1] // 2
    for refs_of, place in ((mine, position), (theirs, 1 - position)):
        for offset, ref in enumerate(refs_of):
            pieces[place, corner ^ offset] = ref[...]
    for ref, place in ((own, position), (other, 1 - position)):
        for side in range(2):
            part = split(ref[:, side * half : (side + 1) * half])
            high[side, place], low[side, place] = part
    grams = []
    for place in range(2):
        first, second = symmetric(pieces[place, 0, :half], pieces[place, 0, half:])
        between = pieces[place, 1, :half]
        grams.append([[first, between], [between.T, second]])
    cross = [
        [pieces[0, 2, :half], pieces[1, 2, :half]],
        [pieces[0, 3, :half], pieces[1, 3, :half]],
    ]
    for step in range(ROUNDS):
        odd = scalars[2 + step] % 2
        turns = []
        for place in range(2):
            (aa, ab), (ba, bb) = grams[place]
            turns.append(split(cayley_of(above(beside(aa, ab), beside(ba, bb)))))
        if step == ROUNDS - 1:
            for place in range(2):
                turn_high[place], turn_low[place] = turns[place]
            for side, place in ((0, position), (1, (position + odd) % 2)):
                held = tuple(beside(x[0, place], x[1, place]) for x in (high, low))
                cols = slice(side * half, (side + 1) * half)
                turn = turn_high[place, :, cols], turn_low[place, :, cols]
                out[:, cols] = dot3(held, turn)
            break
        moved = []
        for place in range(2):
            held = tuple(beside(x[0, place], x[1, place]) for x in (high, low))
            moved.append(dot3(held, turns[place]))
        for place in range(2):
            high[0, place], low[0, place] = split(moved[place][:, :half])
            to = (place + odd) % 2
            high[1, to], low[1, to] = split(moved[place][:, half:])
        new_grams = []
        for place in range(2):
            (aa, ab), (ba, bb) = grams[place]
            gram = above(beside(aa, ab), beside(ba, bb))
            right = dot3(split(gram), turns[place])
            gram = dot3(turns[place], split(right), 0)
            new_grams.append(gram)
        (aa, ab), (ba, bb) = cross
        right = dot3(split(above(beside(aa, ab), beside(ba, bb))), turns[1])
        between = dot3(turns[0], split(right), 0)
        zero, one = new_grams
        swap = odd == 1
        quarters = lambda x: ((x[:half, :half], x[:half, half:]), (x[half:, :half], x[half:, half:]))
        (z_aa, z_ab), (z_ba, z_bb) = quarters(zero)
        (o_aa, o_ab), (o_ba, o_bb) = quarters(one)
        (c_aa, c_ab), (c_ba, c_bb) = quarters(between)
        pick = functools.partial(jnp.where, swap)
        grams = [
            [[z_aa, pick(c_ab, z_ab)], [pick(c_ab.T, z_ba), pick(o_bb, z_bb)]],
            [[o_aa, pick(c_ba.T, o_ab)], [pick(c_ba, o_ba), pick(z_bb, o_bb)]],
        ]
        cross = [[c_aa, pick(z_ab, c_ab)], [pick(o_ba, c_ba), pick(c_bb.T, c_bb)]]


def kernel_of(body, out_shape, ins, scratch=()):
    return pl.pallas_call(
        body,
        out_shape=out_shape,
        in_specs=ins,
        out_specs=jax.tree.map(lambda _: VMEM, out_shape),
        scratch_shapes=list(scratch),
        compiler_params=pltpu.CompilerParams(vmem_limit_bytes=40 * 2**20),
    )


def across(x, mask):
    size = lax.axis_size("rows")
    return lax.ppermute(x, "rows", [(i, i ^ mask) for i in range(size)])


def one_sum(matrix, shifts):
    rows, width = matrix.shape
    half = width // 2
    piece = jax.ShapeDtypeStruct((half + EXTRA, half), F32)
    size = lax.axis_size("rows")
    position = lax.axis_index("pos")
    corner = lax.axis_index("rows") % 4
    where = jnp.stack([position, corner]).astype(jnp.int32)
    other = lax.ppermute(matrix, "pos", [(0, 1), (1, 0)])
    pieces = kernel_of(
        gram_kernel,
        [piece] * 4,
        [SMEM, VMEM, VMEM],
        [
            pltpu.VMEM((2, rows, width), BF16),
            pltpu.VMEM((2, rows, width), BF16),
            pltpu.VMEM((4, half + EXTRA, half), F32),
        ],
    )(where, matrix, other)

    def total(*arrays):
        return kernel_of(sum_kernel, piece, [VMEM] * len(arrays))(*arrays)

    held = total(pieces[0], *[across(pieces[mask], mask) for mask in (1, 2, 3)])
    held = total(held, *[across(held, mask) for mask in range(4, size, 4)])
    mine = [held] + [across(held, mask) for mask in (1, 2, 3)]
    theirs = [lax.ppermute(x, "pos", [(0, 1), (1, 0)]) for x in mine]
    scalars = jnp.concatenate([where, shifts])
    return kernel_of(
        rounds_kernel,
        jax.ShapeDtypeStruct((rows, width), F32),
        [SMEM] + [VMEM] * 10,
        [
            pltpu.VMEM((2, 4, half + EXTRA, half), F32),
            pltpu.VMEM((2, 2, rows, half), BF16),
            pltpu.VMEM((2, 2, rows, half), BF16),
            pltpu.VMEM((2, width, width), BF16),
            pltpu.VMEM((2, width, width), BF16),
        ],
    )(scalars, *mine, *theirs, matrix, other)


def solution(mesh):
    placed = (P("rows", "pos"), P())
    plan = one_sum if mesh.shape["pos"] == 2 and mesh.shape["rows"] == 16 else shards
    return jax.shard_map(
        plan, mesh=mesh, in_specs=placed, out_specs=P("rows", "pos"), check_vma=False
    )
```

```python
import functools

import jax
import jax.numpy as jnp
from jax import lax
from jax.experimental import pallas as pl
from jax.experimental.pallas import tpu as pltpu
from jax.sharding import PartitionSpec as P

ROUNDS = 3
NS_STEPS = 3
EXTRA = 8
CHUNKS = 2
F32 = jnp.float32
BF16 = jnp.bfloat16
VMEM = pl.BlockSpec(memory_space=pltpu.VMEM)
HBM = pl.BlockSpec(memory_space=pltpu.HBM)


def from_behind(x, axis, by):
    size = lax.axis_size(axis)
    return lax.ppermute(x, axis, [(i, (i + by) % size) for i in range(size)])


def product(left, right):
    return jnp.dot(left, right, precision=lax.Precision.HIGHEST, preferred_element_type=F32)


def rotation(gram_matrix):
    width = gram_matrix.shape[0]
    identity = jnp.eye(width, dtype=gram_matrix.dtype)
    inverse_norm = 1.0 / jnp.sqrt(jnp.diagonal(gram_matrix) + 1e-06)
    scaled = gram_matrix * inverse_norm[:, None] * inverse_norm[None, :]
    upper = jnp.triu(scaled, 1)
    skew_raw = upper - upper.T
    bound_value = jnp.max(jnp.sum(jnp.abs(skew_raw), axis=1))
    skew = skew_raw / (1.0 + 2.0 * bound_value)
    shifted = identity - skew
    inverse = identity + skew
    for step in range(NS_STEPS):
        inverse = product(inverse, 2.0 * identity - product(shifted, inverse))
    return product(inverse, identity + skew)


def make_branch(step_size):

    def moved(block):
        if step_size == 0:
            return block
        return from_behind(block, "pos", step_size)

    return moved


def shards(matrix, shifts):
    current = matrix
    half = current.shape[1] // 2
    position_count = lax.axis_size("pos")
    for round_index in range(ROUNDS):
        gram_matrix = lax.psum(product(current.T, current), "rows")
        current = product(current, rotation(gram_matrix))
        distance = shifts[round_index] % position_count
        first_cols = current[:, :half]
        second_cols = current[:, half:]
        branches = [make_branch(step_size) for step_size in range(position_count)]
        second_cols = lax.switch(distance, branches, second_cols)
        current = jnp.concatenate([first_cols, second_cols], axis=1)
    return current


def split(x):
    high = x.astype(BF16)
    return high, (x - high.astype(F32)).astype(BF16)


def dot(left, right, contract=1):
    return lax.dot_general(
        left, right, (((contract,), (0,)), ((), ())), preferred_element_type=F32
    )


def dot3(left, right, contract=1):
    (left_high, left_low), (right_high, right_low) = left, right
    return (
        dot(left_high, right_low, contract)
        + dot(left_low, right_high, contract)
        + dot(left_high, right_high, contract)
    )


def own_kernel(own, high, low, gram, landed, arrived):
    span = own.shape[0] // CHUNKS
    copies = []
    for chunk in range(CHUNKS):
        rows = slice(chunk * span, (chunk + 1) * span)
        copies.append(pltpu.make_async_copy(own.at[rows], landed.at[rows], arrived.at[chunk]))
        copies[-1].start()
    total = None
    for chunk, copy in enumerate(copies):
        rows = slice(chunk * span, (chunk + 1) * span)
        copy.wait()
        parts = split(landed[rows])
        high[rows], low[rows] = parts
        part = dot3(parts, parts, 0)
        total = part if total is None else total + part
    gram[...] = total


def packed(gram):
    half = gram.shape[0] // 2
    first, second = gram[:half, :half], gram[half:, half:]
    row = lax.broadcasted_iota(jnp.int32, (half, half), 0)
    col = lax.broadcasted_iota(jnp.int32, (half, half), 1)
    diagonal = jnp.sum(jnp.where(col == row, second, 0.0), axis=0, keepdims=True)
    return jnp.where(col >= row, first, second), diagonal


def gram_kernel(other, own_high, own_low, own_gram, *refs):
    outs, (high, low, pieces) = refs[:4], refs[4:]
    position = lax.axis_index("pos")
    corner = lax.axis_index("rows") % 4
    half = other.shape[1] // 2
    high[...], low[...] = split(other[...])
    cross = dot3((own_high[...], own_low[...]), (high[...], low[...]), 0)
    first = position == 0
    gram = own_gram[...]
    square, diagonal = packed(gram)
    pieces[0, :half] = square
    pieces[0, half:] = jnp.broadcast_to(diagonal, (EXTRA, half))
    pieces[1, :half] = gram[:half, half:]
    pieces[2, :half] = jnp.where(first, cross[:half, :half], cross[half:, :half])
    pieces[3, :half] = jnp.where(first, cross[half:, :half], cross[half:, half:])
    for piece in (1, 2, 3):
        pieces[piece, half:] = jnp.zeros((EXTRA, half), F32)
    for offset, out in enumerate(outs):
        out[...] = pieces[corner ^ offset]


def sum_kernel(*refs):
    ins, out = refs[:-1], refs[-1]
    total = ins[0][...]
    for ref in ins[1:]:
        total = total + ref[...]
    out[...] = total


def symmetric(block, extra):
    half = block.shape[0]
    row = lax.broadcasted_iota(jnp.int32, (half, half), 0)
    col = lax.broadcasted_iota(jnp.int32, (half, half), 1)
    turned = block.T
    first = jnp.where(col >= row, block, turned)
    second = jnp.where(col > row, turned, jnp.where(col < row, block, extra[:1]))
    return first, second


def beside(left, right):
    return jnp.concatenate([left, right], axis=1)


def above(top, bottom):
    return jnp.concatenate([top, bottom], axis=0)


def skew_of(gram):
    width = gram.shape[0]
    row = lax.broadcasted_iota(jnp.int32, (width, width), 0)
    col = lax.broadcasted_iota(jnp.int32, (width, width), 1)
    on_diagonal = row == col
    diagonal = jnp.where(on_diagonal, gram, 0.0)
    inverse_row = 1.0 / jnp.sqrt(jnp.sum(diagonal, axis=0, keepdims=True) + 1e-06)
    inverse_col = 1.0 / jnp.sqrt(jnp.sum(diagonal, axis=1, keepdims=True) + 1e-06)
    scaled = gram * inverse_col * inverse_row
    raw = jnp.where(on_diagonal, 0.0, jnp.where(col > row, scaled, -scaled))
    bound = jnp.max(jnp.sum(jnp.abs(raw), axis=0, keepdims=True), axis=1, keepdims=True)
    return raw * (1.0 / (1.0 + 2.0 * bound))


def each(function, *lists):
    return [function(*entries) for entries in zip(*lists, strict=True)]


def cayleys_of(grams):
    width = grams[0].shape[0]
    row = lax.broadcasted_iota(jnp.int32, (width, width), 0)
    col = lax.broadcasted_iota(jnp.int32, (width, width), 1)
    identity = jnp.where(row == col, 1.0, 0.0)
    skew = each(skew_of, grams)
    skew_parts = each(split, skew)
    square = each(dot3, skew_parts, skew_parts)
    square_parts = each(split, square)
    fourth = each(dot3, square_parts, square_parts)
    cube = each(dot3, skew_parts, square_parts)
    fourth_parts = each(split, fourth)
    eighth = each(lambda parts: dot(parts[0], parts[0]), fourth_parts)
    base = each(lambda s, y, c, f: identity + 2.0 * (s + y + c) + f, skew, square, cube, fourth)
    base = each(lambda b, parts: b + dot3(split(b), parts), base, fourth_parts)
    return each(lambda b, e: b + dot(b.astype(BF16), e.astype(BF16)), base, eighth)


def whole(blocks):
    return above(beside(*blocks[0]), beside(*blocks[1]))


def quarters(x):
    half = x.shape[0] // 2
    return (x[:half, :half], x[:half, half:]), (x[half:, :half], x[half:, half:])


def rounds_kernel(shifts, *refs):
    mine, theirs, (own_high, own_low, other_high, other_low), out = (
        refs[:4],
        refs[4:8],
        refs[8:12],
        refs[12],
    )
    pieces, high, low, turn_high, turn_low, scalars, arrived = refs[13:]
    fetch = pltpu.make_async_copy(shifts, scalars, arrived)
    fetch.start()
    position = lax.axis_index("pos")
    corner = lax.axis_index("rows") % 4
    width = own_high.shape[1]
    half = width // 2
    for held, place in ((mine, position), (theirs, 1 - position)):
        for offset in range(4):
            pieces[place, corner ^ offset] = held[offset][...]
    for side in range(2):
        cols = slice(side * half, (side + 1) * half)
        high[side, position], low[side, position] = own_high[:, cols], own_low[:, cols]
        high[side, 1 - position], low[side, 1 - position] = other_high[:, cols], other_low[:, cols]
    grams = []
    for place in range(2):
        first, second = symmetric(pieces[place, 0, :half], pieces[place, 0, half:])
        between = pieces[place, 1, :half]
        grams.append([[first, between], [between.T, second]])
    cross = [[pieces[0, 2 + side, :half], pieces[1, 2 + side, :half].T] for side in range(2)]
    fetch.wait()
    for step in range(ROUNDS):
        odd = scalars[step] % 2
        turns = each(split, cayleys_of([whole(blocks) for blocks in grams]))
        if step == ROUNDS - 1:
            for place in range(2):
                turn_high[place], turn_low[place] = turns[place]
            for side, place in ((0, position), (1, (position + odd) % 2)):
                held = tuple(beside(x[0, place], x[1, place]) for x in (high, low))
                cols = slice(side * half, (side + 1) * half)
                turn = turn_high[place, :, cols], turn_low[place, :, cols]
                out[:, cols] = dot3(held, turn)
            break
        full = [whole(blocks) for blocks in grams + [cross]]
        right = each(dot3, each(split, full), [turns[0], turns[1], turns[1]])
        zero, one, between = each(
            lambda turn, parts: dot3(turn, parts, 0),
            [turns[0], turns[1], turns[0]],
            each(split, right),
        )
        pick = functools.partial(jnp.where, odd == 1)
        (z_aa, z_ab), (z_ba, z_bb) = quarters(zero)
        (o_aa, o_ab), (o_ba, o_bb) = quarters(one)
        (c_aa, c_ab), (c_ba, c_bb) = quarters(between)
        grams = [
            [[z_aa, pick(c_ab, z_ab)], [pick(c_ab.T, z_ba), pick(o_bb, z_bb)]],
            [[o_aa, pick(c_ba.T, o_ab)], [pick(c_ba, o_ba), pick(z_bb, o_bb)]],
        ]
        cross = [[c_aa, pick(z_ab, c_ab)], [pick(o_ba, c_ba), pick(c_bb.T, c_bb)]]
        moved = []
        for place in range(2):
            held = tuple(beside(x[0, place], x[1, place]) for x in (high, low))
            moved.append(dot3(held, turns[place]))
        for place in range(2):
            high[0, place], low[0, place] = split(moved[place][:, :half])
            to = (place + odd) % 2
            high[1, to], low[1, to] = split(moved[place][:, half:])


def kernel_of(body, out_shape, ins, scratch=()):
    return pl.pallas_call(
        body,
        out_shape=out_shape,
        in_specs=ins,
        out_specs=jax.tree.map(lambda _: VMEM, out_shape),
        scratch_shapes=list(scratch),
        compiler_params=pltpu.CompilerParams(vmem_limit_bytes=40 * 2**20),
    )


def across(x, mask):
    size = lax.axis_size("rows")
    return lax.ppermute(x, "rows", [(i, i ^ mask) for i in range(size)])


def swapped(x):
    return lax.ppermute(x, "pos", [(0, 1), (1, 0)])


def one_sum(matrix, shifts):
    rows, width = matrix.shape
    half = width // 2
    piece = jax.ShapeDtypeStruct((half + EXTRA, half), F32)
    part = jax.ShapeDtypeStruct((rows, width), BF16)
    square = jax.ShapeDtypeStruct((width, width), F32)
    size = lax.axis_size("rows")
    other = swapped(matrix)
    own_high, own_low, own_gram = kernel_of(
        own_kernel,
        [part, part, square],
        [HBM],
        [pltpu.VMEM(matrix.shape, F32), pltpu.SemaphoreType.DMA((CHUNKS,))],
    )(pltpu.with_memory_space_constraint(matrix, pltpu.HBM))
    *pieces, other_high, other_low = kernel_of(
        gram_kernel,
        [piece] * 4 + [part, part],
        [VMEM] * 4,
        [pltpu.VMEM((4,) + piece.shape, F32)],
    )(other, own_high, own_low, own_gram)

    def total(*arrays):
        return kernel_of(sum_kernel, piece, [VMEM] * len(arrays))(*arrays)

    held = total(pieces[0], *[across(pieces[mask], mask) for mask in (1, 2, 3)])
    held = total(held, *[across(held, mask) for mask in range(4, size, 4)])
    mine = [held] + [across(held, mask) for mask in (1, 2, 3)]
    theirs = [swapped(x) for x in mine]
    return kernel_of(
        rounds_kernel,
        jax.ShapeDtypeStruct((rows, width), F32),
        [HBM] + [VMEM] * 12,
        [
            pltpu.VMEM((2, 4) + piece.shape, F32),
            pltpu.VMEM((2, 2, rows, half), BF16),
            pltpu.VMEM((2, 2, rows, half), BF16),
            pltpu.VMEM((2, width, width), BF16),
            pltpu.VMEM((2, width, width), BF16),
            pltpu.SMEM(shifts.shape, jnp.int32),
            pltpu.SemaphoreType.DMA,
        ],
    )(pltpu.with_memory_space_constraint(shifts, pltpu.HBM), *mine, *theirs, own_high, own_low, other_high, other_low)


def solution(mesh):
    placed = (P("rows", "pos"), P())
    plan = one_sum if mesh.shape["pos"] == 2 and mesh.shape["rows"] == 16 else shards
    return jax.shard_map(
        plan, mesh=mesh, in_specs=placed, out_specs=P("rows", "pos"), check_vma=False
    )
```

```python
import functools

import jax
import jax.numpy as jnp
from jax import lax
from jax.experimental import pallas as pl
from jax.experimental.pallas import tpu as pltpu
from jax.sharding import PartitionSpec as P

ROUNDS = 3
NS_STEPS = 3
EXTRA = 8
CHUNKS = 2
F32 = jnp.float32
BF16 = jnp.bfloat16
VMEM = pl.BlockSpec(memory_space=pltpu.VMEM)
HBM = pl.BlockSpec(memory_space=pltpu.HBM)


def from_behind(x, axis, by):
    size = lax.axis_size(axis)
    return lax.ppermute(x, axis, [(i, (i + by) % size) for i in range(size)])


def product(left, right):
    return jnp.dot(left, right, precision=lax.Precision.HIGHEST, preferred_element_type=F32)


def rotation(gram_matrix):
    width = gram_matrix.shape[0]
    identity = jnp.eye(width, dtype=gram_matrix.dtype)
    inverse_norm = 1.0 / jnp.sqrt(jnp.diagonal(gram_matrix) + 1e-06)
    scaled = gram_matrix * inverse_norm[:, None] * inverse_norm[None, :]
    upper = jnp.triu(scaled, 1)
    skew_raw = upper - upper.T
    bound_value = jnp.max(jnp.sum(jnp.abs(skew_raw), axis=1))
    skew = skew_raw / (1.0 + 2.0 * bound_value)
    shifted = identity - skew
    inverse = identity + skew
    for step in range(NS_STEPS):
        inverse = product(inverse, 2.0 * identity - product(shifted, inverse))
    return product(inverse, identity + skew)


def make_branch(step_size):

    def moved(block):
        if step_size == 0:
            return block
        return from_behind(block, "pos", step_size)

    return moved


def shards(matrix, shifts):
    current = matrix
    half = current.shape[1] // 2
    position_count = lax.axis_size("pos")
    for round_index in range(ROUNDS):
        gram_matrix = lax.psum(product(current.T, current), "rows")
        current = product(current, rotation(gram_matrix))
        distance = shifts[round_index] % position_count
        first_cols = current[:, :half]
        second_cols = current[:, half:]
        branches = [make_branch(step_size) for step_size in range(position_count)]
        second_cols = lax.switch(distance, branches, second_cols)
        current = jnp.concatenate([first_cols, second_cols], axis=1)
    return current


def split(x):
    high = x.astype(BF16)
    return high, (x - high.astype(F32)).astype(BF16)


def dot(left, right, contract=1):
    return lax.dot_general(
        left, right, (((contract,), (0,)), ((), ())), preferred_element_type=F32
    )


def dot3(left, right, contract=1):
    (left_high, left_low), (right_high, right_low) = left, right
    return dot(
        jnp.concatenate([left_high, left_low, left_high], axis=contract),
        jnp.concatenate([right_low, right_high, right_high], axis=0),
        contract,
    )


def own_kernel(own, high, low, gram, landed, arrived):
    span = own.shape[0] // CHUNKS
    copies = []
    for chunk in range(CHUNKS):
        rows = slice(chunk * span, (chunk + 1) * span)
        copies.append(pltpu.make_async_copy(own.at[rows], landed.at[rows], arrived.at[chunk]))
        copies[-1].start()
    total = None
    for chunk, copy in enumerate(copies):
        rows = slice(chunk * span, (chunk + 1) * span)
        copy.wait()
        parts = split(landed[rows])
        high[rows], low[rows] = parts
        part = dot3(parts, parts, 0)
        total = part if total is None else total + part
    gram[...] = total


def packed(gram):
    half = gram.shape[0] // 2
    first, second = gram[:half, :half], gram[half:, half:]
    row = lax.broadcasted_iota(jnp.int32, (half, half), 0)
    col = lax.broadcasted_iota(jnp.int32, (half, half), 1)
    diagonal = jnp.sum(jnp.where(col == row, second, 0.0), axis=0, keepdims=True)
    return jnp.where(col >= row, first, second), diagonal


def gram_kernel(other, own_high, own_low, own_gram, *refs):
    outs, (high, low, pieces) = refs[:4], refs[4:]
    position = lax.axis_index("pos")
    corner = lax.axis_index("rows") % 4
    half = other.shape[1] // 2
    high[...], low[...] = split(other[...])
    cross = dot3((own_high[...], own_low[...]), (high[...], low[...]), 0)
    first = position == 0
    gram = own_gram[...]
    square, diagonal = packed(gram)
    pieces[0, :half] = square
    pieces[0, half:] = jnp.broadcast_to(diagonal, (EXTRA, half))
    pieces[1, :half] = gram[:half, half:]
    pieces[2, :half] = jnp.where(first, cross[:half, :half], cross[half:, :half])
    pieces[3, :half] = jnp.where(first, cross[half:, :half], cross[half:, half:])
    for piece in (1, 2, 3):
        pieces[piece, half:] = jnp.zeros((EXTRA, half), F32)
    for offset, out in enumerate(outs):
        out[...] = pieces[corner ^ offset]


def sum_kernel(*refs):
    ins, out = refs[:-1], refs[-1]
    total = ins[0][...]
    for ref in ins[1:]:
        total = total + ref[...]
    out[...] = total


def symmetric(block, extra):
    half = block.shape[0]
    row = lax.broadcasted_iota(jnp.int32, (half, half), 0)
    col = lax.broadcasted_iota(jnp.int32, (half, half), 1)
    turned = block.T
    first = jnp.where(col >= row, block, turned)
    second = jnp.where(col > row, turned, jnp.where(col < row, block, extra[:1]))
    return first, second


def beside(left, right):
    return jnp.concatenate([left, right], axis=1)


def above(top, bottom):
    return jnp.concatenate([top, bottom], axis=0)


def inverse_norms(block, on_diagonal):
    diagonal = jnp.where(on_diagonal, block, 0.0)
    return tuple(
        1.0 / jnp.sqrt(jnp.sum(diagonal, axis=axis, keepdims=True) + 1e-06) for axis in (1, 0)
    )


def skew_of(blocks):
    (aa, ab), (ba, bb) = blocks
    half = aa.shape[0]
    row = lax.broadcasted_iota(jnp.int32, (half, half), 0)
    col = lax.broadcasted_iota(jnp.int32, (half, half), 1)
    side = jnp.where(col > row, 1.0, jnp.where(col < row, -1.0, 0.0))
    (a_col, a_row), (b_col, b_row) = (inverse_norms(x, col == row) for x in (aa, bb))
    raw = above(
        beside(aa * a_col * a_row * side, ab * a_col * b_row),
        beside(ba * -b_col * a_row, bb * b_col * b_row * side),
    )
    bound = jnp.max(jnp.sum(jnp.abs(raw), axis=0, keepdims=True), axis=1, keepdims=True)
    return raw * (1.0 / (1.0 + 2.0 * bound))


def each(function, *lists):
    return [function(*entries) for entries in zip(*lists, strict=True)]


def cayleys_of(grams):
    width = 2 * grams[0][0][0].shape[0]
    row = lax.broadcasted_iota(jnp.int32, (width, width), 0)
    col = lax.broadcasted_iota(jnp.int32, (width, width), 1)
    identity = jnp.where(row == col, 1.0, 0.0)
    skew = each(skew_of, grams)
    skew_parts = each(split, skew)
    square = each(dot3, skew_parts, skew_parts)
    square_parts = each(split, square)
    fourth = each(dot3, square_parts, square_parts)
    cube = each(dot3, skew_parts, square_parts)
    fourth_parts = each(split, fourth)
    eighth = each(lambda parts: dot(parts[0], parts[0]), fourth_parts)
    base = each(lambda s, y, c, f: identity + 2.0 * (s + y + c) + f, skew, square, cube, fourth)
    base = each(
        lambda b, f, parts: b + f + dot((b - identity).astype(BF16), parts[0]),
        base,
        fourth,
        fourth_parts,
    )
    return each(
        lambda b, e: b + e + dot((b - identity).astype(BF16), e.astype(BF16)), base, eighth
    )


def whole(blocks):
    return above(beside(*blocks[0]), beside(*blocks[1]))


def quarters(x):
    half = x.shape[0] // 2
    return (x[:half, :half], x[:half, half:]), (x[half:, :half], x[half:, half:])


def rounds_kernel(shifts, *refs):
    mine, theirs, (own_high, own_low, other_high, other_low), out = (
        refs[:4],
        refs[4:8],
        refs[8:12],
        refs[12],
    )
    pieces, high, low, turn_high, turn_low, scalars, arrived = refs[13:]
    fetch = pltpu.make_async_copy(shifts, scalars, arrived)
    fetch.start()
    position = lax.axis_index("pos")
    corner = lax.axis_index("rows") % 4
    width = own_high.shape[1]
    half = width // 2
    for held, place in ((mine, position), (theirs, 1 - position)):
        for offset in range(4):
            pieces[place, corner ^ offset] = held[offset][...]
    for side in range(2):
        cols = slice(side * half, (side + 1) * half)
        high[side, position], low[side, position] = own_high[:, cols], own_low[:, cols]
        high[side, 1 - position], low[side, 1 - position] = other_high[:, cols], other_low[:, cols]
    grams = []
    for place in range(2):
        first, second = symmetric(pieces[place, 0, :half], pieces[place, 0, half:])
        between = pieces[place, 1, :half]
        grams.append([[first, between], [between.T, second]])
    cross = [[pieces[0, 2 + side, :half], pieces[1, 2 + side, :half].T] for side in range(2)]
    for step in range(ROUNDS):
        turns = each(split, cayleys_of(grams))
        if step == ROUNDS - 1:
            odd = scalars[step] % 2
            for place in range(2):
                turn_high[place], turn_low[place] = turns[place]
            for side, place in ((0, position), (1, (position + odd) % 2)):
                held = tuple(beside(x[0, place], x[1, place]) for x in (high, low))
                cols = slice(side * half, (side + 1) * half)
                turn = turn_high[place, :, cols], turn_low[place, :, cols]
                out[:, cols] = dot3(held, turn)
            break
        full = [whole(blocks) for blocks in grams + [cross]]
        right = each(dot3, each(split, full), [turns[0], turns[1], turns[1]])
        zero, one, between = each(
            lambda turn, parts: dot3(turn, parts, 0),
            [turns[0], turns[1], turns[0]],
            each(split, right),
        )
        if step == 0:
            fetch.wait()
        odd = scalars[step] % 2
        pick = functools.partial(jnp.where, odd == 1)
        (z_aa, z_ab), (z_ba, z_bb) = quarters(zero)
        (o_aa, o_ab), (o_ba, o_bb) = quarters(one)
        (c_aa, c_ab), (c_ba, c_bb) = quarters(between)
        grams = [
            [[z_aa, pick(c_ab, z_ab)], [pick(c_ab.T, z_ba), pick(o_bb, z_bb)]],
            [[o_aa, pick(c_ba.T, o_ab)], [pick(c_ba, o_ba), pick(z_bb, o_bb)]],
        ]
        cross = [[c_aa, pick(z_ab, c_ab)], [pick(o_ba, c_ba), pick(c_bb.T, c_bb)]]
        moved = []
        for place in range(2):
            held = tuple(beside(x[0, place], x[1, place]) for x in (high, low))
            moved.append(dot3(held, turns[place]))
        for place in range(2):
            high[0, place], low[0, place] = split(moved[place][:, :half])
            to = (place + odd) % 2
            high[1, to], low[1, to] = split(moved[place][:, half:])


def kernel_of(body, out_shape, ins, scratch=()):
    return pl.pallas_call(
        body,
        out_shape=out_shape,
        in_specs=ins,
        out_specs=jax.tree.map(lambda _: VMEM, out_shape),
        scratch_shapes=list(scratch),
        compiler_params=pltpu.CompilerParams(vmem_limit_bytes=40 * 2**20),
    )


def across(x, mask):
    size = lax.axis_size("rows")
    return lax.ppermute(x, "rows", [(i, i ^ mask) for i in range(size)])


def swapped(x):
    return lax.ppermute(x, "pos", [(0, 1), (1, 0)])


def one_sum(matrix, shifts):
    rows, width = matrix.shape
    half = width // 2
    piece = jax.ShapeDtypeStruct((half + EXTRA, half), F32)
    part = jax.ShapeDtypeStruct((rows, width), BF16)
    square = jax.ShapeDtypeStruct((width, width), F32)
    size = lax.axis_size("rows")
    other = swapped(matrix)
    own_high, own_low, own_gram = kernel_of(
        own_kernel,
        [part, part, square],
        [HBM],
        [pltpu.VMEM(matrix.shape, F32), pltpu.SemaphoreType.DMA((CHUNKS,))],
    )(pltpu.with_memory_space_constraint(matrix, pltpu.HBM))
    *pieces, other_high, other_low = kernel_of(
        gram_kernel,
        [piece] * 4 + [part, part],
        [VMEM] * 4,
        [pltpu.VMEM((4,) + piece.shape, F32)],
    )(other, own_high, own_low, own_gram)

    def total(*arrays):
        return kernel_of(sum_kernel, piece, [VMEM] * len(arrays))(*arrays)

    held = total(pieces[0], *[across(pieces[mask], mask) for mask in (1, 2, 3)])
    held = total(held, *[across(held, mask) for mask in range(4, size, 4)])
    mine = [held] + [across(held, mask) for mask in (1, 2, 3)]
    theirs = [swapped(x) for x in mine]
    return kernel_of(
        rounds_kernel,
        jax.ShapeDtypeStruct((rows, width), F32),
        [HBM] + [VMEM] * 12,
        [
            pltpu.VMEM((2, 4) + piece.shape, F32),
            pltpu.VMEM((2, 2, rows, half), BF16),
            pltpu.VMEM((2, 2, rows, half), BF16),
            pltpu.VMEM((2, width, width), BF16),
            pltpu.VMEM((2, width, width), BF16),
            pltpu.SMEM(shifts.shape, jnp.int32),
            pltpu.SemaphoreType.DMA,
        ],
    )(pltpu.with_memory_space_constraint(shifts, pltpu.HBM), *mine, *theirs, own_high, own_low, other_high, other_low)


def solution(mesh):
    placed = (P("rows", "pos"), P())
    plan = one_sum if mesh.shape["pos"] == 2 and mesh.shape["rows"] == 16 else shards
    return jax.shard_map(
        plan, mesh=mesh, in_specs=placed, out_specs=P("rows", "pos"), check_vma=False
    )
```

```python
import functools

import jax
import jax.numpy as jnp
from jax import lax
from jax.experimental import pallas as pl
from jax.experimental.pallas import tpu as pltpu
from jax.sharding import PartitionSpec as P

ROUNDS = 3
NS_STEPS = 3
EXTRA = 8
CHUNKS = 2
PAIRS = {
    (2, 2): ((0, 1), (1, 0), (0, 0)),
    (2, 3): ((1, 1), (0, 2), (0, 1), (1, 0), (0, 0)),
    (3, 2): ((1, 1), (2, 0), (0, 1), (1, 0), (0, 0)),
    (3, 3): ((1, 1), (0, 2), (2, 0), (0, 1), (1, 0), (0, 0)),
}
F32 = jnp.float32
BF16 = jnp.bfloat16
VMEM = pl.BlockSpec(memory_space=pltpu.VMEM)
HBM = pl.BlockSpec(memory_space=pltpu.HBM)


def from_behind(x, axis, by):
    size = lax.axis_size(axis)
    return lax.ppermute(x, axis, [(i, (i + by) % size) for i in range(size)])


def product(left, right):
    return jnp.dot(left, right, precision=lax.Precision.HIGHEST, preferred_element_type=F32)


def rotation(gram_matrix):
    width = gram_matrix.shape[0]
    identity = jnp.eye(width, dtype=gram_matrix.dtype)
    inverse_norm = 1.0 / jnp.sqrt(jnp.diagonal(gram_matrix) + 1e-06)
    scaled = gram_matrix * inverse_norm[:, None] * inverse_norm[None, :]
    upper = jnp.triu(scaled, 1)
    skew_raw = upper - upper.T
    bound_value = jnp.max(jnp.sum(jnp.abs(skew_raw), axis=1))
    skew = skew_raw / (1.0 + 2.0 * bound_value)
    shifted = identity - skew
    inverse = identity + skew
    for step in range(NS_STEPS):
        inverse = product(inverse, 2.0 * identity - product(shifted, inverse))
    return product(inverse, identity + skew)


def make_branch(step_size):

    def moved(block):
        if step_size == 0:
            return block
        return from_behind(block, "pos", step_size)

    return moved


def shards(matrix, shifts):
    current = matrix
    half = current.shape[1] // 2
    position_count = lax.axis_size("pos")
    for round_index in range(ROUNDS):
        gram_matrix = lax.psum(product(current.T, current), "rows")
        current = product(current, rotation(gram_matrix))
        distance = shifts[round_index] % position_count
        first_cols = current[:, :half]
        second_cols = current[:, half:]
        branches = [make_branch(step_size) for step_size in range(position_count)]
        second_cols = lax.switch(distance, branches, second_cols)
        current = jnp.concatenate([first_cols, second_cols], axis=1)
    return current


def split(x, parts=2):
    made = []
    for part in range(parts):
        made.append(x.astype(BF16))
        if part < parts - 1:
            x = x - made[-1].astype(F32)
    return tuple(made)


def dot(left, right, contract=1):
    return lax.dot_general(
        left, right, (((contract,), (0,)), ((), ())), preferred_element_type=F32
    )


def dots(left, right, contract=1):
    pairs = PAIRS[len(left), len(right)]
    return dot(
        jnp.concatenate([left[a] for a, _ in pairs], axis=contract),
        jnp.concatenate([right[b] for _, b in pairs], axis=0),
        contract,
    )


def own_kernel(own, high, low, rest, gram, landed, arrived):
    span = own.shape[0] // CHUNKS
    copies = []
    for chunk in range(CHUNKS):
        rows = slice(chunk * span, (chunk + 1) * span)
        copies.append(pltpu.make_async_copy(own.at[rows], landed.at[rows], arrived.at[chunk]))
        copies[-1].start()
    total = None
    for chunk, copy in enumerate(copies):
        rows = slice(chunk * span, (chunk + 1) * span)
        copy.wait()
        parts = split(landed[rows], 3)
        high[rows], low[rows], rest[rows] = parts
        part = dots(parts, parts, 0)
        total = part if total is None else total + part
    gram[...] = total


def packed(gram):
    half = gram.shape[0] // 2
    first, second = gram[:half, :half], gram[half:, half:]
    row = lax.broadcasted_iota(jnp.int32, (half, half), 0)
    col = lax.broadcasted_iota(jnp.int32, (half, half), 1)
    diagonal = jnp.sum(jnp.where(col == row, second, 0.0), axis=0, keepdims=True)
    return jnp.where(col >= row, first, second), diagonal


def gram_kernel(other, own_high, own_low, own_rest, own_gram, *refs):
    outs, (high, low, pieces) = refs[:4], refs[4:]
    position = lax.axis_index("pos")
    corner = lax.axis_index("rows") % 4
    half = other.shape[1] // 2
    parts = split(other[...], 3)
    high[...], low[...] = parts[:2]
    cross = dots((own_high[...], own_low[...], own_rest[...]), parts, 0)
    first = position == 0
    gram = own_gram[...]
    square, diagonal = packed(gram)
    pieces[0, :half] = square
    pieces[0, half:] = jnp.broadcast_to(diagonal, (EXTRA, half))
    pieces[1, :half] = gram[:half, half:]
    pieces[2, :half] = jnp.where(first, cross[:half, :half], cross[half:, :half])
    pieces[3, :half] = jnp.where(first, cross[half:, :half], cross[half:, half:])
    for piece in (1, 2, 3):
        pieces[piece, half:] = jnp.zeros((EXTRA, half), F32)
    for offset, out in enumerate(outs):
        out[...] = pieces[corner ^ offset]


def sum_kernel(*refs):
    ins, out = refs[:-1], refs[-1]
    total = ins[0][...]
    for ref in ins[1:]:
        total = total + ref[...]
    out[...] = total


def symmetric(block, extra):
    half = block.shape[0]
    row = lax.broadcasted_iota(jnp.int32, (half, half), 0)
    col = lax.broadcasted_iota(jnp.int32, (half, half), 1)
    turned = block.T
    first = jnp.where(col >= row, block, turned)
    second = jnp.where(col > row, turned, jnp.where(col < row, block, extra[:1]))
    return first, second


def beside(left, right):
    return jnp.concatenate([left, right], axis=1)


def above(top, bottom):
    return jnp.concatenate([top, bottom], axis=0)


def inverse_norms(block, on_diagonal):
    diagonal = jnp.where(on_diagonal, block, 0.0)
    return tuple(
        1.0 / jnp.sqrt(jnp.maximum(jnp.sum(diagonal, axis=axis, keepdims=True), 0.0) + 1e-06)
        for axis in (1, 0)
    )


def raw_of(blocks):
    (aa, ab), (ba, bb) = blocks
    half = aa.shape[0]
    row = lax.broadcasted_iota(jnp.int32, (half, half), 0)
    col = lax.broadcasted_iota(jnp.int32, (half, half), 1)
    side = jnp.where(col > row, 1.0, jnp.where(col < row, -1.0, 0.0))
    (a_col, a_row), (b_col, b_row) = (inverse_norms(x, col == row) for x in (aa, bb))
    bounded = functools.partial(jnp.clip, min=-1.0, max=1.0)
    raw = above(
        beside(bounded(aa * a_col * a_row) * side, bounded(ab * a_col * b_row)),
        beside(bounded(ba * -b_col * a_row), bounded(bb * b_col * b_row) * side),
    )
    bound = jnp.max(jnp.sum(jnp.abs(raw), axis=0, keepdims=True), axis=1, keepdims=True)
    return raw, 1.0 / (1.0 + 2.0 * bound)


def each(function, *lists):
    return [function(*entries) for entries in zip(*lists, strict=True)]


def cayleys_of(grams):
    width = 2 * grams[0][0][0].shape[0]
    row = lax.broadcasted_iota(jnp.int32, (width, width), 0)
    col = lax.broadcasted_iota(jnp.int32, (width, width), 1)
    identity = jnp.where(row == col, 1.0, 0.0)
    raw, scale = zip(*each(raw_of, grams), strict=True)
    raw_parts = each(split, raw)
    square = each(lambda parts, c: dots(parts, parts) * (c * c), raw_parts, scale)
    square_parts = each(split, square)
    fourth = each(dots, square_parts, square_parts)
    cube = each(dots, raw_parts, square_parts)
    fourth_parts = each(split, fourth)
    eighth = each(lambda parts: dot(parts[0], parts[0]), fourth_parts)
    base = each(
        lambda r, k, y, c, f: identity + 2.0 * ((r + c) * k + y) + f,
        raw,
        scale,
        square,
        cube,
        fourth,
    )
    base = each(
        lambda b, f, parts: b + f + dot((b - identity).astype(BF16), parts[0]),
        base,
        fourth,
        fourth_parts,
    )
    return each(
        lambda b, e: b + e + dot((b - identity).astype(BF16), e.astype(BF16)), base, eighth
    )


def whole(blocks):
    return above(beside(*blocks[0]), beside(*blocks[1]))


def quarters(x):
    half = x.shape[0] // 2
    return (x[:half, :half], x[:half, half:]), (x[half:, :half], x[half:, half:])


def rounds_kernel(shifts, *refs):
    mine, theirs, (own_high, own_low, other_high, other_low), out = (
        refs[:4],
        refs[4:8],
        refs[8:12],
        refs[12],
    )
    pieces, high, low, turn_high, turn_low, scalars, arrived = refs[13:]
    fetch = pltpu.make_async_copy(shifts, scalars, arrived)
    fetch.start()
    position = lax.axis_index("pos")
    corner = lax.axis_index("rows") % 4
    width = own_high.shape[1]
    half = width // 2
    for held, place in ((mine, position), (theirs, 1 - position)):
        for offset in range(4):
            pieces[place, corner ^ offset] = held[offset][...]
    for side in range(2):
        cols = slice(side * half, (side + 1) * half)
        high[side, position], low[side, position] = own_high[:, cols], own_low[:, cols]
        high[side, 1 - position], low[side, 1 - position] = other_high[:, cols], other_low[:, cols]
    grams = []
    for place in range(2):
        first, second = symmetric(pieces[place, 0, :half], pieces[place, 0, half:])
        between = pieces[place, 1, :half]
        grams.append([[first, between], [between.T, second]])
    cross = [[pieces[0, 2 + side, :half], pieces[1, 2 + side, :half].T] for side in range(2)]
    for step in range(ROUNDS):
        turns = each(split, cayleys_of(grams))
        if step == ROUNDS - 1:
            odd = scalars[step] % 2
            for place in range(2):
                turn_high[place], turn_low[place] = turns[place]
            for side, place in ((0, position), (1, (position + odd) % 2)):
                held = tuple(beside(x[0, place], x[1, place]) for x in (high, low))
                cols = slice(side * half, (side + 1) * half)
                turn = turn_high[place, :, cols], turn_low[place, :, cols]
                out[:, cols] = dots(held, turn)
            break
        full = [whole(blocks) for blocks in grams + [cross]]
        right = each(dots, each(functools.partial(split, parts=3), full), [turns[0], turns[1], turns[1]])
        zero, one, between = each(
            lambda turn, parts: dots(turn, parts, 0),
            [turns[0], turns[1], turns[0]],
            each(functools.partial(split, parts=3), right),
        )
        if step == 0:
            fetch.wait()
        odd = scalars[step] % 2
        pick = functools.partial(jnp.where, odd == 1)
        (z_aa, z_ab), (z_ba, z_bb) = quarters(zero)
        (o_aa, o_ab), (o_ba, o_bb) = quarters(one)
        (c_aa, c_ab), (c_ba, c_bb) = quarters(between)
        grams = [
            [[z_aa, pick(c_ab, z_ab)], [pick(c_ab.T, z_ba), pick(o_bb, z_bb)]],
            [[o_aa, pick(c_ba.T, o_ab)], [pick(c_ba, o_ba), pick(z_bb, o_bb)]],
        ]
        cross = [[c_aa, pick(z_ab, c_ab)], [pick(o_ba, c_ba), pick(c_bb.T, c_bb)]]
        moved = []
        for place in range(2):
            held = tuple(beside(x[0, place], x[1, place]) for x in (high, low))
            moved.append(dots(held, turns[place]))
        for place in range(2):
            high[0, place], low[0, place] = split(moved[place][:, :half])
            to = (place + odd) % 2
            high[1, to], low[1, to] = split(moved[place][:, half:])


def kernel_of(body, out_shape, ins, scratch=()):
    return pl.pallas_call(
        body,
        out_shape=out_shape,
        in_specs=ins,
        out_specs=jax.tree.map(lambda _: VMEM, out_shape),
        scratch_shapes=list(scratch),
        compiler_params=pltpu.CompilerParams(vmem_limit_bytes=40 * 2**20),
    )


def across(x, mask):
    size = lax.axis_size("rows")
    return lax.ppermute(x, "rows", [(i, i ^ mask) for i in range(size)])


def swapped(x):
    return lax.ppermute(x, "pos", [(0, 1), (1, 0)])


def one_sum(matrix, shifts):
    rows, width = matrix.shape
    half = width // 2
    piece = jax.ShapeDtypeStruct((half + EXTRA, half), F32)
    part = jax.ShapeDtypeStruct((rows, width), BF16)
    square = jax.ShapeDtypeStruct((width, width), F32)
    size = lax.axis_size("rows")
    other = swapped(matrix)
    own_high, own_low, own_rest, own_gram = kernel_of(
        own_kernel,
        [part, part, part, square],
        [HBM],
        [pltpu.VMEM(matrix.shape, F32), pltpu.SemaphoreType.DMA((CHUNKS,))],
    )(pltpu.with_memory_space_constraint(matrix, pltpu.HBM))
    *pieces, other_high, other_low = kernel_of(
        gram_kernel,
        [piece] * 4 + [part, part],
        [VMEM] * 5,
        [pltpu.VMEM((4,) + piece.shape, F32)],
    )(other, own_high, own_low, own_rest, own_gram)

    def total(*arrays):
        return kernel_of(sum_kernel, piece, [VMEM] * len(arrays))(*arrays)

    held = total(pieces[0], *[across(pieces[mask], mask) for mask in (1, 2, 3)])
    held = total(held, *[across(held, mask) for mask in range(4, size, 4)])
    mine = [held] + [across(held, mask) for mask in (1, 2, 3)]
    theirs = [swapped(x) for x in mine]
    return kernel_of(
        rounds_kernel,
        jax.ShapeDtypeStruct((rows, width), F32),
        [HBM] + [VMEM] * 12,
        [
            pltpu.VMEM((2, 4) + piece.shape, F32),
            pltpu.VMEM((2, 2, rows, half), BF16),
            pltpu.VMEM((2, 2, rows, half), BF16),
            pltpu.VMEM((2, width, width), BF16),
            pltpu.VMEM((2, width, width), BF16),
            pltpu.SMEM(shifts.shape, jnp.int32),
            pltpu.SemaphoreType.DMA,
        ],
    )(pltpu.with_memory_space_constraint(shifts, pltpu.HBM), *mine, *theirs, own_high, own_low, other_high, other_low)


def solution(mesh):
    placed = (P("rows", "pos"), P())
    plan = one_sum if mesh.shape["pos"] == 2 and mesh.shape["rows"] == 16 else shards
    return jax.shard_map(
        plan, mesh=mesh, in_specs=placed, out_specs=P("rows", "pos"), check_vma=False
    )
```

```python
import functools

import jax
import jax.numpy as jnp
from jax import lax
from jax.experimental import pallas as pl
from jax.experimental.pallas import tpu as pltpu
from jax.sharding import PartitionSpec as P

ROUNDS = 3
NS_STEPS = 3
EXTRA = 8
CHUNKS = 2
PAIRS = {
    (2, 2): ((0, 1), (1, 0), (0, 0)),
    (2, 3): ((1, 1), (0, 2), (0, 1), (1, 0), (0, 0)),
    (3, 2): ((1, 1), (2, 0), (0, 1), (1, 0), (0, 0)),
    (3, 3): ((1, 1), (0, 2), (2, 0), (0, 1), (1, 0), (0, 0)),
}
F32 = jnp.float32
BF16 = jnp.bfloat16
VMEM = pl.BlockSpec(memory_space=pltpu.VMEM)
HBM = pl.BlockSpec(memory_space=pltpu.HBM)


def from_behind(x, axis, by):
    size = lax.axis_size(axis)
    return lax.ppermute(x, axis, [(i, (i + by) % size) for i in range(size)])


def product(left, right):
    return jnp.dot(left, right, precision=lax.Precision.HIGHEST, preferred_element_type=F32)


def rotation(gram_matrix):
    width = gram_matrix.shape[0]
    identity = jnp.eye(width, dtype=gram_matrix.dtype)
    inverse_norm = 1.0 / jnp.sqrt(jnp.diagonal(gram_matrix) + 1e-06)
    scaled = gram_matrix * inverse_norm[:, None] * inverse_norm[None, :]
    upper = jnp.triu(scaled, 1)
    skew_raw = upper - upper.T
    bound_value = jnp.max(jnp.sum(jnp.abs(skew_raw), axis=1))
    skew = skew_raw / (1.0 + 2.0 * bound_value)
    shifted = identity - skew
    inverse = identity + skew
    for step in range(NS_STEPS):
        inverse = product(inverse, 2.0 * identity - product(shifted, inverse))
    return product(inverse, identity + skew)


def make_branch(step_size):

    def moved(block):
        if step_size == 0:
            return block
        return from_behind(block, "pos", step_size)

    return moved


def shards(matrix, shifts):
    current = matrix
    half = current.shape[1] // 2
    position_count = lax.axis_size("pos")
    for round_index in range(ROUNDS):
        gram_matrix = lax.psum(product(current.T, current), "rows")
        current = product(current, rotation(gram_matrix))
        distance = shifts[round_index] % position_count
        first_cols = current[:, :half]
        second_cols = current[:, half:]
        branches = [make_branch(step_size) for step_size in range(position_count)]
        second_cols = lax.switch(distance, branches, second_cols)
        current = jnp.concatenate([first_cols, second_cols], axis=1)
    return current


def split(x, parts=2):
    made = []
    for part in range(parts):
        made.append(x.astype(BF16))
        if part < parts - 1:
            x = x - made[-1].astype(F32)
    return tuple(made)


def dot(left, right, contract=1):
    return lax.dot_general(
        left, right, (((contract,), (0,)), ((), ())), preferred_element_type=F32
    )


def dots(left, right, contract=1):
    pairs = PAIRS[len(left), len(right)]
    return dot(
        jnp.concatenate([left[a] for a, _ in pairs], axis=contract),
        jnp.concatenate([right[b] for _, b in pairs], axis=0),
        contract,
    )


def own_kernel(own, high, low, rest, gram, landed, arrived):
    span = own.shape[0] // CHUNKS
    copies = []
    for chunk in range(CHUNKS):
        rows = slice(chunk * span, (chunk + 1) * span)
        copies.append(pltpu.make_async_copy(own.at[rows], landed.at[rows], arrived.at[chunk]))
        copies[-1].start()
    total = None
    for chunk, copy in enumerate(copies):
        rows = slice(chunk * span, (chunk + 1) * span)
        copy.wait()
        parts = split(landed[rows], 3)
        high[rows], low[rows], rest[rows] = parts
        part = dots(parts, parts, 0)
        total = part if total is None else total + part
    gram[...] = total


def packed(gram):
    half = gram.shape[0] // 2
    first, second = gram[:half, :half], gram[half:, half:]
    row = lax.broadcasted_iota(jnp.int32, (half, half), 0)
    col = lax.broadcasted_iota(jnp.int32, (half, half), 1)
    diagonal = jnp.sum(jnp.where(col == row, second, 0.0), axis=0, keepdims=True)
    return jnp.where(col >= row, first, second), diagonal


def gram_kernel(other, own_high, own_low, own_rest, own_gram, *refs):
    outs, (high, low, pieces) = refs[:4], refs[4:]
    position = lax.axis_index("pos")
    corner = lax.axis_index("rows") % 4
    half = other.shape[1] // 2
    parts = split(other[...], 3)
    high[...], low[...] = parts[:2]
    cross = dots((own_high[...], own_low[...], own_rest[...]), parts, 0)
    first = position == 0
    gram = own_gram[...]
    square, diagonal = packed(gram)
    pieces[0, :half] = square
    pieces[0, half:] = jnp.broadcast_to(diagonal, (EXTRA, half))
    pieces[1, :half] = gram[:half, half:]
    pieces[2, :half] = jnp.where(first, cross[:half, :half], cross[half:, :half])
    pieces[3, :half] = jnp.where(first, cross[half:, :half], cross[half:, half:])
    for piece in (1, 2, 3):
        pieces[piece, half:] = jnp.zeros((EXTRA, half), F32)
    for offset, out in enumerate(outs):
        out[...] = pieces[corner ^ offset]


def sum_kernel(*refs):
    ins, out = refs[:-1], refs[-1]
    total = ins[0][...]
    for ref in ins[1:]:
        total = total + ref[...]
    out[...] = total


def symmetric(block, extra):
    half = block.shape[0]
    row = lax.broadcasted_iota(jnp.int32, (half, half), 0)
    col = lax.broadcasted_iota(jnp.int32, (half, half), 1)
    turned = block.T
    first = jnp.where(col >= row, block, turned)
    second = jnp.where(col > row, turned, jnp.where(col < row, block, extra[:1]))
    return first, second


def beside(left, right):
    return jnp.concatenate([left, right], axis=1)


def above(top, bottom):
    return jnp.concatenate([top, bottom], axis=0)


def inverse_norms(block, on_diagonal):
    diagonal = jnp.where(on_diagonal, block, 0.0)
    return tuple(
        1.0 / jnp.sqrt(jnp.maximum(jnp.sum(diagonal, axis=axis, keepdims=True), 0.0) + 1e-06)
        for axis in (1, 0)
    )


def raw_of(blocks):
    (aa, ab), (ba, bb) = blocks
    half = aa.shape[0]
    row = lax.broadcasted_iota(jnp.int32, (half, half), 0)
    col = lax.broadcasted_iota(jnp.int32, (half, half), 1)
    side = jnp.where(col > row, 1.0, jnp.where(col < row, -1.0, 0.0))
    (a_col, a_row), (b_col, b_row) = (inverse_norms(x, col == row) for x in (aa, bb))
    bounded = functools.partial(jnp.clip, min=-1.0, max=1.0)
    raw = above(
        beside(bounded(aa * a_col * a_row) * side, bounded(ab * a_col * b_row)),
        beside(bounded(ba * -b_col * a_row), bounded(bb * b_col * b_row) * side),
    )
    bound = jnp.max(jnp.sum(jnp.abs(raw), axis=0, keepdims=True), axis=1, keepdims=True)
    return raw, 1.0 / (1.0 + 2.0 * bound)


def each(function, *lists):
    return [function(*entries) for entries in zip(*lists, strict=True)]


def cayleys_of(grams):
    width = 2 * grams[0][0][0].shape[0]
    row = lax.broadcasted_iota(jnp.int32, (width, width), 0)
    col = lax.broadcasted_iota(jnp.int32, (width, width), 1)
    identity = jnp.where(row == col, 1.0, 0.0)
    raw, scale = zip(*each(raw_of, grams), strict=True)
    raw_parts = each(split, raw)
    square = each(lambda parts, c: dots(parts, parts) * (c * c), raw_parts, scale)
    square_parts = each(split, square)
    fourth = each(dots, square_parts, square_parts)
    cube = each(dots, raw_parts, square_parts)
    fourth_parts = each(split, fourth)
    eighth = each(lambda parts: dot(parts[0], parts[0]), fourth_parts)
    base = each(
        lambda r, k, y, c, f: identity + 2.0 * ((r + c) * k + y) + f,
        raw,
        scale,
        square,
        cube,
        fourth,
    )
    base = each(
        lambda b, f, parts: b + f + dot((b - identity).astype(BF16), parts[0]),
        base,
        fourth,
        fourth_parts,
    )
    return each(
        lambda b, e: b + e + dot((b - identity).astype(BF16), e.astype(BF16)), base, eighth
    )


def whole(blocks):
    return above(beside(*blocks[0]), beside(*blocks[1]))


def quarters(x):
    half = x.shape[0] // 2
    return (x[:half, :half], x[:half, half:]), (x[half:, :half], x[half:, half:])


def rounds_kernel(shifts, *refs):
    mine, theirs, (own_high, own_low, other_high, other_low), out = (
        refs[:4],
        refs[4:8],
        refs[8:12],
        refs[12],
    )
    pieces, high, low, turn_high, turn_low, scalars, arrived = refs[13:]
    fetch = pltpu.make_async_copy(shifts, scalars, arrived)
    fetch.start()
    position = lax.axis_index("pos")
    corner = lax.axis_index("rows") % 4
    width = own_high.shape[1]
    half = width // 2
    for held, place in ((mine, position), (theirs, 1 - position)):
        for offset in range(4):
            pieces[place, corner ^ offset] = held[offset][...]
    for side in range(2):
        cols = slice(side * half, (side + 1) * half)
        high[side, position], low[side, position] = own_high[:, cols], own_low[:, cols]
        high[side, 1 - position], low[side, 1 - position] = other_high[:, cols], other_low[:, cols]
    grams = []
    for place in range(2):
        first, second = symmetric(pieces[place, 0, :half], pieces[place, 0, half:])
        between = pieces[place, 1, :half]
        grams.append([[first, between], [between.T, second]])
    cross = [[pieces[0, 2 + side, :half], pieces[1, 2 + side, :half].T] for side in range(2)]
    for step in range(ROUNDS):
        turns = each(split, cayleys_of(grams))
        if step == ROUNDS - 1:
            odd = scalars[step] % 2
            for place in range(2):
                turn_high[place], turn_low[place] = turns[place]
            for side, place in ((0, position), (1, (position + odd) % 2)):
                held = tuple(beside(x[0, place], x[1, place]) for x in (high, low))
                cols = slice(side * half, (side + 1) * half)
                turn = turn_high[place, :, cols], turn_low[place, :, cols]
                out[:, cols] = dots(held, turn)
            break
        full = [whole(blocks) for blocks in grams + [cross]]
        right = each(dots, each(functools.partial(split, parts=3), full), [turns[0], turns[1], turns[1]])
        zero, one, between = each(
            lambda turn, parts: dots(turn, parts, 0),
            [turns[0], turns[1], turns[0]],
            each(functools.partial(split, parts=2 if step else 3), right),
        )
        if step == 0:
            fetch.wait()
        odd = scalars[step] % 2
        pick = functools.partial(jnp.where, odd == 1)
        (z_aa, z_ab), (z_ba, z_bb) = quarters(zero)
        (o_aa, o_ab), (o_ba, o_bb) = quarters(one)
        (c_aa, c_ab), (c_ba, c_bb) = quarters(between)
        grams = [
            [[z_aa, pick(c_ab, z_ab)], [pick(c_ab.T, z_ba), pick(o_bb, z_bb)]],
            [[o_aa, pick(c_ba.T, o_ab)], [pick(c_ba, o_ba), pick(z_bb, o_bb)]],
        ]
        cross = [[c_aa, pick(z_ab, c_ab)], [pick(o_ba, c_ba), pick(c_bb.T, c_bb)]]
        moved = []
        for place in range(2):
            held = tuple(beside(x[0, place], x[1, place]) for x in (high, low))
            moved.append(dots(held, turns[place]))
        for place in range(2):
            high[0, place], low[0, place] = split(moved[place][:, :half])
            to = (place + odd) % 2
            high[1, to], low[1, to] = split(moved[place][:, half:])


def kernel_of(body, out_shape, ins, scratch=()):
    return pl.pallas_call(
        body,
        out_shape=out_shape,
        in_specs=ins,
        out_specs=jax.tree.map(lambda _: VMEM, out_shape),
        scratch_shapes=list(scratch),
        compiler_params=pltpu.CompilerParams(vmem_limit_bytes=40 * 2**20),
    )


def across(x, mask):
    size = lax.axis_size("rows")
    return lax.ppermute(x, "rows", [(i, i ^ mask) for i in range(size)])


def swapped(x):
    return lax.ppermute(x, "pos", [(0, 1), (1, 0)])


def one_sum(matrix, shifts):
    rows, width = matrix.shape
    half = width // 2
    piece = jax.ShapeDtypeStruct((half + EXTRA, half), F32)
    part = jax.ShapeDtypeStruct((rows, width), BF16)
    square = jax.ShapeDtypeStruct((width, width), F32)
    size = lax.axis_size("rows")
    other = swapped(matrix)
    own_high, own_low, own_rest, own_gram = kernel_of(
        own_kernel,
        [part, part, part, square],
        [HBM],
        [pltpu.VMEM(matrix.shape, F32), pltpu.SemaphoreType.DMA((CHUNKS,))],
    )(pltpu.with_memory_space_constraint(matrix, pltpu.HBM))
    *pieces, other_high, other_low = kernel_of(
        gram_kernel,
        [piece] * 4 + [part, part],
        [VMEM] * 5,
        [pltpu.VMEM((4,) + piece.shape, F32)],
    )(other, own_high, own_low, own_rest, own_gram)

    def total(*arrays):
        return kernel_of(sum_kernel, piece, [VMEM] * len(arrays))(*arrays)

    held = total(pieces[0], *[across(pieces[mask], mask) for mask in (1, 2, 3)])
    held = total(held, *[across(held, mask) for mask in range(4, size, 4)])
    mine = [held] + [across(held, mask) for mask in (1, 2, 3)]
    theirs = [swapped(x) for x in mine]
    return kernel_of(
        rounds_kernel,
        jax.ShapeDtypeStruct((rows, width), F32),
        [HBM] + [VMEM] * 12,
        [
            pltpu.VMEM((2, 4) + piece.shape, F32),
            pltpu.VMEM((2, 2, rows, half), BF16),
            pltpu.VMEM((2, 2, rows, half), BF16),
            pltpu.VMEM((2, width, width), BF16),
            pltpu.VMEM((2, width, width), BF16),
            pltpu.SMEM(shifts.shape, jnp.int32),
            pltpu.SemaphoreType.DMA,
        ],
    )(pltpu.with_memory_space_constraint(shifts, pltpu.HBM), *mine, *theirs, own_high, own_low, other_high, other_low)


def solution(mesh):
    placed = (P("rows", "pos"), P())
    plan = one_sum if mesh.shape["pos"] == 2 and mesh.shape["rows"] == 16 else shards
    return jax.shard_map(
        plan, mesh=mesh, in_specs=placed, out_specs=P("rows", "pos"), check_vma=False
    )
```
